512 devices in a mesh: gx: 16 (over z_lo, x), gy: 4 (over y), gz: 8 (over z_hi, core).
Axes of the slice: x: 4, y: 4, z: 16 (z_hi: 4, z_lo: 4; z = z_hi * 4 + z_lo), core: 2. Of those that a mesh axis runs over, the one named last changes fastest.
Arguments:
- tensor: float32 [32, 512, 32, 512], P(None, 'gx', 'gz', 'gy'), may hold values from -11 to 11, as said below
- factor: float32 [512, 64], P('gx'), may hold values from -0.25 to 0.25
Outputs:
- core_tensor: float32 [32, 64, 32, 512], P('gx', None, 'gz', 'gy')
- gram_matrix: float32 [512, 512], P('gy')
The draws below stay inside these ranges and needn't reach their ends.
Inputs may be any that keep to these rules, and one draw needn't show every extreme that they name: `tensor`: real-valued field, rough from cell to cell.
All inputs are finite; a program needn't handle non-finite values.
Results may differ from the reference program's by a relative error of at most 0.00012.
Values sent between devices are 32-bit elements; how exact they have to be, the bound alone decides.
No kernel may reach another device: no remote copies, remote signals or barrier semaphores. Data moves between devices by JAX's collectives and lax.ppermute only.
A program may use at most 64 MiB of HBM per device.

```python
import jax
import jax.numpy as jnp
from jax import lax

V = 32
R = 64
NX = 512
NY = 512
NZ = 32


def draw_tensor(key, part):
    key = jax.random.fold_in(key, 7)
    key_base, key_gain, key_noise = jax.random.split(key, 3)
    column_gain = jax.random.uniform(key_gain, (1, 1, 1, NY), jnp.float32, 0.5, 1.5)
    base_field = jax.random.truncated_normal(key_base, -4.0, 4.0, (V, NX, NZ, 1), jnp.float32)
    noise_field = jax.random.truncated_normal(key_noise, -4.0, 4.0, (V, NX, NZ, NY), jnp.float32)
    values = 0.8 * base_field * column_gain + 0.6 * noise_field
    return values.astype(jnp.float32)


def steps_of(key, dims, cuts, low, top_value):
    loudness, own = 1.0, jax.random.fold_in(key, 6)
    for dim, shards_of in cuts:
        heights = jnp.exp(jax.random.uniform(jax.random.fold_in(own, dim), (shards_of,), jnp.float32, low / len(cuts), top_value / len(cuts)))
        loudness = loudness * jnp.repeat(heights, dims[dim] // shards_of).reshape([-1 if axis == dim else 1 for axis in range(len(dims))])
    return loudness


def normal_values(own_key, dims, scale, limit, cuts=(), dtype=jnp.bfloat16):
    drawn = scale * jax.random.normal(own_key, dims, jnp.float32)
    if cuts:
        drawn = drawn * steps_of(own_key, dims, cuts, -0.22, 0.18)
    return jnp.clip(drawn, -limit, limit).astype(dtype)


def setup_inputs(seed: int = 0) -> dict:
    splits = jax.random.split(jax.random.key(seed), 3)
    return {
        "tensor": draw_tensor(jax.random.fold_in(splits[2], 71), 0),
        "factor": normal_values(splits[1], (NX, R), NX ** -0.5, 0.25, ((0, 16),), jnp.float32),
    }


def reference(tensor, factor):
    core_tensor = jnp.einsum('ir,vikj->vrkj', factor, tensor, precision=lax.Precision.HIGHEST)
    gram_matrix = jnp.einsum('vrkj,vrkl->jl', core_tensor, core_tensor, precision=lax.Precision.HIGHEST)
    gram_matrix = gram_matrix / jnp.float32(V * R * NZ)
    return core_tensor, gram_matrix
```

```python
import jax
import jax.numpy as jnp
from jax import lax
from jax.sharding import Mesh, PartitionSpec as P

HIGH = lax.Precision.HIGHEST


def exchange(a, axes):
    return lax.all_to_all(a, axes, 0, 0)


def copies(a, count):
    return jnp.broadcast_to(a[None], (count, *a.shape))


def local(tensor, factor):
    v, i, k, j = tensor.shape
    r = factor.shape[1]
    nx, nzl, ny, nzh, nc = (lax.axis_size(a) for a in ("x", "zl", "y", "zh", "c"))

    share, mine = v // nx, v // (nx * nzl)
    rows = i * r // (k * j)
    field = tensor.reshape(nzl, nx, mine * i, k, j).swapaxes(0, 1).reshape(nx, share * i, k, j)
    sent = jnp.concatenate([field, copies(factor.reshape(rows, k, j), nx)], axis=1)
    got = exchange(sent, "x")
    field = got[:, : share * i].reshape(nx, share, i, k, j)
    rows_of = got[:, share * i :].reshape(nx, i, r)
    products = jnp.einsum("xir,xvikj->vrkj", rows_of, field, precision=HIGH)

    core = exchange(products.reshape(nzl, mine, r, k, j), "zl").sum(axis=0)

    slices = exchange(copies(core, ny), "y")
    gram = jnp.einsum("vrkj,yvrkl->jyl", core, slices, precision=HIGH).reshape(j, ny * j)
    gram = gram * (1.0 / float(v * r * k * nzh * nc))

    group = ("zl", "x", "c")
    count = nzl * nx * nc
    part = exchange(gram.reshape(count, -1, ny * j), group).sum(axis=0)
    part = exchange(copies(part, nzh), "zh").sum(axis=0)
    gram = exchange(copies(part, count), group).reshape(j, ny * j)
    return core, gram


def solution(mesh):
    fine = Mesh(mesh.devices.reshape(4, 4, 4, 4, 2), ("zl", "x", "y", "zh", "c"))
    gx, gz = ("zl", "x"), ("zh", "c")
    in_specs = (P(None, gx, gz, "y"), P(gx, None))
    out_specs = (P(gx, None, gz, "y"), P("y", None))
    return jax.shard_map(local, mesh=fine, in_specs=in_specs, out_specs=out_specs, check_vma=False)
```

```python
import jax
import jax.numpy as jnp
from jax import lax
from jax.sharding import Mesh, PartitionSpec as P

HIGH = lax.Precision.HIGH
ZL = ("zm", "zn")
LANES = 128
LATE = 3


def exchange(a, axes):
    return lax.all_to_all(a, axes, 0, 0)


def copies(a, count):
    return jnp.broadcast_to(a[None], (count, *a.shape))


def pick(a, index):
    return lax.dynamic_index_in_dim(a, index, 0)


def local(tensor, factor):
    v, i, k, j = tensor.shape
    r = factor.shape[1]
    nx, nzl, ny, nzh, nc = (lax.axis_size(a) for a in ("x", ZL, "y", "zh", "c"))
    me_x, me_z = lax.axis_index("x"), lax.axis_index(ZL)
    mine = v // (nx * nzl)
    slabs = tensor.reshape(nzl, nx, mine, i, k, j).swapaxes(3, 4).reshape(nzl, nx, mine * k, i, j)
    factor = jnp.pad(factor, ((0, 0), (0, LANES - r)))

    late = slabs[:, :, -LATE:].reshape(nzl, -1, j)
    late = jnp.concatenate([late, copies(factor, nzl)], axis=1)
    came = exchange(late, ZL)
    rest = slabs[:, :, :-LATE].swapaxes(0, 1).reshape(nx, -1, j)
    rest = jnp.concatenate([rest, copies(factor, nx)], axis=1)
    got = [pick(rest, me_x)]
    for d in (2, 1, 3):
        got.append(lax.ppermute(pick(rest, (me_x + d) % nx), "x", [(x, (x + d) % nx) for x in range(nx)]))
    got = jnp.concatenate(got)

    def product(got):
        field = got[:, :-i].reshape(nx, -1, i, j)
        return jnp.einsum("xir,xuij->urj", got[:, -i:, :r], field, precision=HIGH)

    products = product(got).reshape(nzl, -1, r, j)
    products, came = lax.optimization_barrier((products, came))
    other = product(came).reshape(nx, -1, r, j)

    sums = exchange(products, ZL).sum(axis=0)
    tail = pick(other, me_x)[0]
    for d in (2, 1, 3):
        tail = tail + lax.ppermute(pick(other, (me_x + d) % nx), "x", [(x, (x + d) % nx) for x in range(nx)])[0]
    core = jnp.concatenate([sums, tail]).reshape(-1, j)

    slices = exchange(copies(core, ny), "y")
    gram = jnp.einsum("aj,yal->jyl", core, slices, precision=HIGH).reshape(j, ny * j)
    gram = gram * (1.0 / float(v * r * k * nzh * nc))

    near, far = ("x", "c", "zn"), ("zm", "zh")
    count, others = nx * nc * nzl // 2, 2 * nzh
    part = exchange(gram.reshape(count, -1, ny * j), near).sum(axis=0)
    part = exchange(copies(part, others), far).sum(axis=0)
    gram = exchange(copies(part, count), near).reshape(j, ny * j)
    return core.reshape(mine, k, r, j).swapaxes(1, 2), gram


def solution(mesh):
    fine = Mesh(mesh.devices.reshape(2, 2, 4, 4, 4, 2), ("zm", "zn", "x", "y", "zh", "c"))
    gx, gz = (*ZL, "x"), ("zh", "c")
    in_specs = (P(None, gx, gz, "y"), P(gx, None))
    out_specs = (P(gx, None, gz, "y"), P("y", None))
    return jax.shard_map(local, mesh=fine, in_specs=in_specs, out_specs=out_specs, check_vma=False)
```

```python
import jax
import jax.numpy as jnp
from jax import lax
from jax.sharding import Mesh, PartitionSpec as P

HIGH = lax.Precision.HIGH
ZL = ("zm", "zn")
LANES = 128
LATE = 3


def exchange(a, axes):
    return lax.all_to_all(a, axes, 0, 0)


def copies(a, count):
    return jnp.broadcast_to(a[None], (count, *a.shape))


def pick(a, index):
    return lax.dynamic_index_in_dim(a, index, 0)


def local(tensor, factor):
    v, i, k, j = tensor.shape
    r = factor.shape[1]
    nx, nzl, ny, nzh, nc = (lax.axis_size(a) for a in ("x", ZL, "y", "zh", "c"))
    me_x, me_z = lax.axis_index("x"), lax.axis_index(ZL)
    mine = v // (nx * nzl)
    late = tensor.reshape(nzl, nx, mine, i, k, j)[:, :, 1, :, k - LATE :].swapaxes(2, 3)
    late, tensor = lax.optimization_barrier((late, tensor))
    slabs = tensor.reshape(nzl, nx, mine, i, k, j).swapaxes(3, 4).reshape(nzl, nx, mine * k, i, j)
    factor = jnp.pad(factor, ((0, 0), (0, LANES - r)))

    late = late.reshape(nzl, -1, j)
    late = jnp.concatenate([late, copies(factor, nzl)], axis=1)
    came = exchange(late, ZL)
    rest = slabs[:, :, :-LATE].swapaxes(0, 1).reshape(nx, -1, j)
    rest = jnp.concatenate([rest, copies(factor, nx)], axis=1)
    got = [pick(rest, me_x)]
    for d in (1, 3, 2):
        got.append(lax.ppermute(pick(rest, (me_x + d) % nx), "x", [(x, (x + d) % nx) for x in range(nx)]))
    got = jnp.concatenate(got)

    def product(got):
        field = got[:, :-i].reshape(nx, -1, i, j)
        return jnp.einsum("xir,xuij->urj", got[:, -i:, :r], field, precision=HIGH)

    products = product(got).reshape(nzl, -1, r, j)
    products, came = lax.optimization_barrier((products, came))
    other = product(came).reshape(nx, -1, r, j)

    sums = exchange(products, ZL).sum(axis=0)
    tail = pick(other, me_x)[0]
    for d in (2, 1, 3):
        tail = tail + lax.ppermute(pick(other, (me_x + d) % nx), "x", [(x, (x + d) % nx) for x in range(nx)])[0]
    core = jnp.concatenate([sums, tail]).reshape(-1, j)

    slices = exchange(copies(core, ny), "y")
    gram = jnp.einsum("aj,yal->jyl", core, slices, precision=HIGH).reshape(j, ny * j)
    gram = gram * (1.0 / float(v * r * k * nzh * nc))

    near, far = ("x", "c", "zn"), ("zm", "zh")
    count, others = nx * nc * nzl // 2, 2 * nzh
    part = exchange(gram.reshape(count, -1, ny * j), near).sum(axis=0)
    part = exchange(copies(part, others), far).sum(axis=0)
    gram = exchange(copies(part, count), near).reshape(j, ny * j)
    return core.reshape(mine, k, r, j).swapaxes(1, 2), gram


def solution(mesh):
    fine = Mesh(mesh.devices.reshape(2, 2, 4, 4, 4, 2), ("zm", "zn", "x", "y", "zh", "c"))
    gx, gz = (*ZL, "x"), ("zh", "c")
    in_specs = (P(None, gx, gz, "y"), P(gx, None))
    out_specs = (P(gx, None, gz, "y"), P("y", None))
    return jax.shard_map(local, mesh=fine, in_specs=in_specs, out_specs=out_specs, check_vma=False)
```

```python
import jax
import jax.numpy as jnp
from jax import lax
from jax.sharding import Mesh, PartitionSpec as P

HIGH, HIGHEST = lax.Precision.HIGH, lax.Precision.HIGHEST
ZL = ("zm", "zn")
LANES = 128
LATE = 3


def exchange(a, axes):
    return lax.all_to_all(a, axes, 0, 0)


def copies(a, count):
    return jnp.broadcast_to(a[None], (count, *a.shape))


def pick(a, index):
    return lax.dynamic_index_in_dim(a, index, 0)


def local(tensor, factor):
    v, i, k, j = tensor.shape
    r = factor.shape[1]
    nx, nzl, ny, nzh, nc = (lax.axis_size(a) for a in ("x", ZL, "y", "zh", "c"))
    me_x, me_z = lax.axis_index("x"), lax.axis_index(ZL)
    mine = v // (nx * nzl)
    late = tensor.reshape(nzl, nx, mine, i, k, j)[:, :, 1, :, k - LATE :].swapaxes(2, 3)
    late, tensor = lax.optimization_barrier((late, tensor))
    slabs = tensor.reshape(nzl, nx, mine, i, k, j).swapaxes(3, 4).reshape(nzl, nx, mine * k, i, j)
    factor = jnp.pad(factor, ((0, 0), (0, LANES - r)))

    late = late.reshape(nzl, -1, j)
    late = jnp.concatenate([late, copies(factor, nzl)], axis=1)
    came = exchange(late, ZL)
    rest = slabs[:, :, :-LATE].swapaxes(0, 1).reshape(nx, -1, j)
    rest = jnp.concatenate([rest, copies(factor, nx)], axis=1)
    got = [pick(rest, me_x)]
    for d in (1, 3, 2):
        got.append(lax.ppermute(pick(rest, (me_x + d) % nx), "x", [(x, (x + d) % nx) for x in range(nx)]))
    got = jnp.concatenate(got)

    def product(got):
        field = got[:, :-i].reshape(nx, -1, i, j)
        return jnp.einsum("xir,xuij->urj", got[:, -i:, :r], field, precision=HIGHEST)

    products = product(got).reshape(nzl, -1, r, j)
    other = product(came).reshape(nx, -1, r, j)

    sums = exchange(products, ZL).sum(axis=0)
    tail = pick(other, me_x)[0]
    for d in (1, 3, 2):
        tail = tail + lax.ppermute(pick(other, (me_x + d) % nx), "x", [(x, (x + d) % nx) for x in range(nx)])[0]
    core = jnp.concatenate([sums, tail]).reshape(-1, j)

    slices = exchange(copies(core, ny), "y")
    gram = jnp.einsum("aj,yal->jyl", core, slices, precision=HIGH).reshape(j, ny * j)
    gram = gram * (1.0 / float(v * r * k * nzh * nc))

    near, far = ("zn", "x", "c"), ("zm", "zh")
    count, others = nx * nc * nzl // 2, 2 * nzh
    part = exchange(gram.reshape(count, -1, ny * j), near).sum(axis=0)
    part = exchange(copies(part, others), far).sum(axis=0)
    gram = exchange(copies(part, count), near).reshape(j, ny * j)
    return core.reshape(mine, k, r, j).swapaxes(1, 2), gram


def solution(mesh):
    fine = Mesh(mesh.devices.reshape(2, 2, 4, 4, 4, 2), ("zm", "zn", "x", "y", "zh", "c"))
    gx, gz = (*ZL, "x"), ("zh", "c")
    in_specs = (P(None, gx, gz, "y"), P(gx, None))
    out_specs = (P(gx, None, gz, "y"), P("y", None))
    return jax.shard_map(local, mesh=fine, in_specs=in_specs, out_specs=out_specs, check_vma=False)
```

```python
import jax
import jax.numpy as jnp
from jax import lax
from jax.sharding import Mesh, PartitionSpec as P

HIGH, HIGHEST = lax.Precision.HIGH, lax.Precision.HIGHEST
ZL = ("zm", "zn")
LANES = 128
LATE = 3


def exchange(a, axes):
    return lax.all_to_all(a, axes, 0, 0)


def copies(a, count):
    return jnp.broadcast_to(a[None], (count, *a.shape))


def pick(a, index):
    return lax.dynamic_index_in_dim(a, index, 0)


def local(tensor, factor):
    v, i, k, j = tensor.shape
    r = factor.shape[1]
    nx, nzl, ny, nzh, nc = (lax.axis_size(a) for a in ("x", ZL, "y", "zh", "c"))
    me_x, me_z = lax.axis_index("x"), lax.axis_index(ZL)
    mine = v // (nx * nzl)
    late = tensor.reshape(nzl, nx, mine, i, k, j)[:, :, 1, :, k - LATE :].swapaxes(2, 3)
    late, tensor = lax.optimization_barrier((late, tensor))
    slabs = tensor.reshape(nzl, nx, mine, i, k, j).swapaxes(3, 4).reshape(nzl, nx, mine * k, i, j)
    factor = jnp.pad(factor, ((0, 0), (0, LANES - r)))

    late = late.reshape(nzl, -1, j)
    late = jnp.concatenate([late, copies(factor, nzl)], axis=1)
    came = exchange(late, ZL)
    rest = slabs[:, :, :-LATE].swapaxes(0, 1).reshape(nx, -1, j)
    rest = jnp.concatenate([rest, copies(factor, nx)], axis=1)
    got = [pick(rest, me_x)]
    for d in (1, 3, 2):
        got.append(lax.ppermute(pick(rest, (me_x + d) % nx), "x", [(x, (x + d) % nx) for x in range(nx)]))

    def product(got):
        field = got[:, :-i].reshape(got.shape[0], -1, i, j)
        return jnp.einsum("xir,xuij->urj", got[:, -i:, :r], field, precision=HIGHEST)

    products = (product(jnp.concatenate(got[:-1])) + product(got[-1])).reshape(nzl, -1, r, j)
    other = product(came).reshape(nx, -1, r, j)

    sums = exchange(products, ZL).sum(axis=0)
    tail = pick(other, me_x)[0]
    for d in (1, 3, 2):
        tail = tail + lax.ppermute(pick(other, (me_x + d) % nx), "x", [(x, (x + d) % nx) for x in range(nx)])[0]
    core = jnp.concatenate([sums, tail]).reshape(-1, j)

    slices = exchange(copies(core, ny), "y")
    gram = jnp.einsum("aj,yal->jyl", core, slices, precision=HIGH).reshape(j, ny * j)
    gram = gram * (1.0 / float(v * r * k * nzh * nc))

    near, far = ("zn", "x", "c"), ("zm", "zh")
    count, others = nx * nc * nzl // 2, 2 * nzh
    part = exchange(gram.reshape(count, -1, ny * j), near).sum(axis=0)
    part = exchange(copies(part, others), far).sum(axis=0)
    gram = exchange(copies(part, count), near).reshape(j, ny * j)
    return core.reshape(mine, k, r, j).swapaxes(1, 2), gram


def solution(mesh):
    fine = Mesh(mesh.devices.reshape(2, 2, 4, 4, 4, 2), ("zm", "zn", "x", "y", "zh", "c"))
    gx, gz = (*ZL, "x"), ("zh", "c")
    in_specs = (P(None, gx, gz, "y"), P(gx, None))
    out_specs = (P(gx, None, gz, "y"), P("y", None))
    return jax.shard_map(local, mesh=fine, in_specs=in_specs, out_specs=out_specs, check_vma=False)
```

```python
import jax
import jax.numpy as jnp
from jax import lax
from jax.sharding import Mesh, PartitionSpec as P

HIGH, HIGHEST = lax.Precision.HIGH, lax.Precision.HIGHEST
ZL = ("zm", "zn")
LANES = 128
LATE = 3


def exchange(a, axes):
    return lax.all_to_all(a, axes, 0, 0)


def copies(a, count):
    return jnp.broadcast_to(a[None], (count, *a.shape))


def pick(a, index):
    return lax.dynamic_index_in_dim(a, index, 0)


def local(tensor, factor):
    v, i, k, j = tensor.shape
    r = factor.shape[1]
    nx, nzl, ny, nzh, nc = (lax.axis_size(a) for a in ("x", ZL, "y", "zh", "c"))
    me_x, me_z = lax.axis_index("x"), lax.axis_index(ZL)
    mine = v // (nx * nzl)
    late = tensor.reshape(nzl, nx, mine, i, k, j)[:, :, 1, :, k - LATE :].swapaxes(2, 3)
    late, tensor = lax.optimization_barrier((late, tensor))
    slabs = tensor.reshape(nzl, nx, mine, i, k, j).swapaxes(3, 4).reshape(nzl, nx, mine * k, i, j)
    factor = jnp.pad(factor, ((0, 0), (0, LANES - r)))

    late = late.reshape(nzl, -1, j)
    late = jnp.concatenate([late, copies(factor, nzl)], axis=1)
    came = exchange(late, ZL)
    rest = slabs[:, :, :-LATE].swapaxes(0, 1).reshape(nx, -1, j)
    rest = jnp.concatenate([rest, copies(factor, nx)], axis=1)
    got = [pick(rest, me_x)]
    for d in (1, 3, 2):
        got.append(lax.ppermute(pick(rest, (me_x + d) % nx), "x", [(x, (x + d) % nx) for x in range(nx)]))

    def product(got):
        field = got[:, :-i].reshape(got.shape[0], -1, i, j)
        return jnp.einsum("xir,xuij->urj", got[:, -i:, :r], field, precision=HIGHEST)

    products, last = lax.optimization_barrier((product(jnp.concatenate(got[:-1])), got[-1]))
    products = (products + product(last)).reshape(nzl, -1, r, j)
    other = product(came).reshape(nx, -1, r, j)

    sums = exchange(products, ZL).sum(axis=0)
    tail = pick(other, me_x)[0]
    for d in (1, 3, 2):
        tail = tail + lax.ppermute(pick(other, (me_x + d) % nx), "x", [(x, (x + d) % nx) for x in range(nx)])[0]
    core = jnp.concatenate([sums, tail]).reshape(-1, j)

    slices = exchange(copies(core, ny), "y")
    gram = jnp.einsum("aj,yal->jyl", core, slices, precision=HIGH).reshape(j, ny * j)
    gram = gram * (1.0 / float(v * r * k * nzh * nc))

    near, far = ("zn", "x", "c"), ("zm", "zh")
    count, others = nx * nc * nzl // 2, 2 * nzh
    part = exchange(gram.reshape(count, -1, ny * j), near).sum(axis=0)
    part = exchange(copies(part, others), far).sum(axis=0)
    gram = exchange(copies(part, count), near).reshape(j, ny * j)
    return core.reshape(mine, k, r, j).swapaxes(1, 2), gram


def solution(mesh):
    fine = Mesh(mesh.devices.reshape(2, 2, 4, 4, 4, 2), ("zm", "zn", "x", "y", "zh", "c"))
    gx, gz = (*ZL, "x"), ("zh", "c")
    in_specs = (P(None, gx, gz, "y"), P(gx, None))
    out_specs = (P(gx, None, gz, "y"), P("y", None))
    return jax.shard_map(local, mesh=fine, in_specs=in_specs, out_specs=out_specs, check_vma=False)
```

```python
import jax
import jax.numpy as jnp
from jax import lax
from jax.sharding import Mesh, PartitionSpec as P

HIGH, HIGHEST = lax.Precision.HIGH, lax.Precision.HIGHEST
ZL = ("zm", "zn")
LATE = 3


def exchange(a, axes):
    return lax.all_to_all(a, axes, 0, 0)


def copies(a, count):
    return jnp.broadcast_to(a[None], (count, *a.shape))


def pick(a, index):
    return lax.dynamic_index_in_dim(a, index, 0)


def local(tensor, factor):
    v, i, k, j = tensor.shape
    r = factor.shape[1]
    nx, nzl, ny, nzh, nc = (lax.axis_size(a) for a in ("x", ZL, "y", "zh", "c"))
    me_x, me_z = lax.axis_index("x"), lax.axis_index(ZL)
    mine = v // (nx * nzl)
    late = tensor.reshape(nzl, nx, mine, i, k, j)[:, :, 1, :, k - LATE :].swapaxes(2, 3)
    late, tensor = lax.optimization_barrier((late, tensor))
    slabs = tensor.reshape(nzl, nx, mine, i, k, j).swapaxes(3, 4).reshape(nzl, nx, mine * k, i, j)
    factor = jnp.concatenate([factor[: i // 2], factor[i // 2 :]], axis=1)

    late = late.reshape(nzl, -1, j)
    late = jnp.concatenate([late, copies(factor, nzl)], axis=1)
    came = exchange(late, ZL)
    rest = slabs[:, :, :-LATE].swapaxes(0, 1).reshape(nx, -1, j)
    rest = jnp.concatenate([rest, copies(factor, nx)], axis=1)
    got = [pick(rest, me_x)]
    for d in (1, 3, 2):
        got.append(lax.ppermute(pick(rest, (me_x + d) % nx), "x", [(x, (x + d) % nx) for x in range(nx)]))

    def product(got):
        field = got[:, : -i // 2].reshape(got.shape[0], -1, i, j)
        rows_of = jnp.concatenate([got[:, -i // 2 :, :r], got[:, -i // 2 :, r:]], axis=1)
        return jnp.einsum("xir,xuij->urj", rows_of, field, precision=HIGHEST)

    products, last = lax.optimization_barrier((product(jnp.concatenate(got[:-1])), got[-1]))
    products = (products + product(last)).reshape(nzl, -1, r, j)
    other = product(came).reshape(nx, -1, r, j)

    sums = exchange(products, ZL).sum(axis=0)
    tail = pick(other, me_x)[0]
    for d in (1, 3, 2):
        tail = tail + lax.ppermute(pick(other, (me_x + d) % nx), "x", [(x, (x + d) % nx) for x in range(nx)])[0]
    core = jnp.concatenate([sums, tail]).reshape(-1, j)

    slices = exchange(copies(core, ny), "y")
    gram = jnp.einsum("aj,yal->jyl", core, slices, precision=HIGH).reshape(j, ny * j)
    gram = gram * (1.0 / float(v * r * k * nzh * nc))

    near, far = ("zn", "x", "c"), ("zm", "zh")
    count, others = nx * nc * nzl // 2, 2 * nzh
    part = exchange(gram.reshape(count, -1, ny * j), near).sum(axis=0)
    part = exchange(copies(part, others), far).sum(axis=0)
    gram = exchange(copies(part, count), near).reshape(j, ny * j)
    return core.reshape(mine, k, r, j).swapaxes(1, 2), gram


def solution(mesh):
    fine = Mesh(mesh.devices.reshape(2, 2, 4, 4, 4, 2), ("zm", "zn", "x", "y", "zh", "c"))
    gx, gz = (*ZL, "x"), ("zh", "c")
    in_specs = (P(None, gx, gz, "y"), P(gx, None))
    out_specs = (P(gx, None, gz, "y"), P("y", None))
    return jax.shard_map(local, mesh=fine, in_specs=in_specs, out_specs=out_specs, check_vma=False)
```

```python
import jax
import jax.numpy as jnp
from jax import lax
from jax.sharding import Mesh, PartitionSpec as P

HIGH, HIGHEST = lax.Precision.HIGH, lax.Precision.HIGHEST
ZL = ("zm", "zn")
LATE = 3


def exchange(a, axes):
    return lax.all_to_all(a, axes, 0, 0)


def copies(a, count):
    return jnp.broadcast_to(a[None], (count, *a.shape))


def pick(a, index):
    return lax.dynamic_index_in_dim(a, index, 0)


def local(tensor, factor):
    v, i, k, j = tensor.shape
    r = factor.shape[1]
    nx, nzl, ny, nzh, nc = (lax.axis_size(a) for a in ("x", ZL, "y", "zh", "c"))
    me_x, me_z = lax.axis_index("x"), lax.axis_index(ZL)
    mine = v // (nx * nzl)
    late = tensor.reshape(nzl, nx, mine, i, k, j)[:, :, 1, :, k - LATE :].swapaxes(2, 3)
    late, tensor = lax.optimization_barrier((late, tensor))
    slabs = tensor.reshape(nzl, nx, mine, i, k, j).swapaxes(3, 4).reshape(nzl, nx, mine * k, i, j)
    factor = jnp.concatenate([factor[: i // 2], factor[i // 2 :]], axis=1)

    late = late.reshape(nzl, -1, j)
    late = jnp.concatenate([late, copies(factor, nzl)], axis=1)
    came = exchange(late, ZL)
    rest = slabs[:, :, :-LATE].swapaxes(0, 1).reshape(nx, -1, j)
    rest = jnp.concatenate([rest, copies(factor, nx)], axis=1)
    got = [pick(rest, me_x)]
    for d in (1, 3, 2):
        got.append(lax.ppermute(pick(rest, (me_x + d) % nx), "x", [(x, (x + d) % nx) for x in range(nx)]))

    def product(got):
        field = got[:, : -i // 2].reshape(got.shape[0], -1, i, j)
        rows_of = jnp.concatenate([got[:, -i // 2 :, :r], got[:, -i // 2 :, r:]], axis=1)
        return jnp.einsum("xir,xuij->urj", rows_of, field, precision=HIGHEST)

    products, other, last = lax.optimization_barrier((product(jnp.concatenate(got[:-1])), product(came), got[-1]))
    other = other.reshape(nx, -1, r, j)
    products = (products + product(last)).reshape(nzl, -1, r, j)

    sums = exchange(products, ZL).sum(axis=0)
    tail = pick(other, me_x)[0]
    for d in (1, 3, 2):
        tail = tail + lax.ppermute(pick(other, (me_x + d) % nx), "x", [(x, (x + d) % nx) for x in range(nx)])[0]
    core = jnp.concatenate([sums, tail]).reshape(-1, j)

    slices = exchange(copies(core, ny), "y")
    gram = jnp.einsum("aj,yal->jyl", core, slices, precision=HIGH).reshape(j, ny * j)
    gram = gram * (1.0 / float(v * r * k * nzh * nc))

    near, far = ("zn", "x", "c"), ("zm", "zh")
    count, others = nx * nc * nzl // 2, 2 * nzh
    part = exchange(gram.reshape(count, -1, ny * j), near).sum(axis=0)
    part = exchange(copies(part, others), far).sum(axis=0)
    gram = exchange(copies(part, count), near).reshape(j, ny * j)
    return core.reshape(mine, k, r, j).swapaxes(1, 2), gram


def solution(mesh):
    fine = Mesh(mesh.devices.reshape(2, 2, 4, 4, 4, 2), ("zm", "zn", "x", "y", "zh", "c"))
    gx, gz = (*ZL, "x"), ("zh", "c")
    in_specs = (P(None, gx, gz, "y"), P(gx, None))
    out_specs = (P(gx, None, gz, "y"), P("y", None))
    return jax.shard_map(local, mesh=fine, in_specs=in_specs, out_specs=out_specs, check_vma=False)
```
